32 devices in a mesh: dp: 4 (over z), row: 2 (over x), col: 4 (over y, core).
Axes of the slice: x: 2, y: 2, z: 4, core: 2. Of those that a mesh axis runs over, the one named last changes fastest.
Arguments:
- tokens: bfloat16 [8, 256, 768], P('dp', None, 'row'), may hold values from -6 to 6
- condition: bfloat16 [8, 768], P('dp', 'col'), may hold values from -5 to 5
- cotangent: bfloat16 [8, 256, 768], P('dp', None, 'row'), may hold values from -6 to 6
- w_ada: bfloat16 [2, 768, 6, 768], P(None, 'col', None, 'row'), may hold values from -0.21875 to 0.21875
- b_ada: bfloat16 [2, 6, 768], P(None, None, 'row'), may hold values from -1.5 to 1.5
- w_qkv: bfloat16 [2, 768, 3, 768], P(None, 'row', None, 'col'), may hold values from -0.21875 to 0.21875
- b_qv: bfloat16 [2, 2, 768], P(None, None, 'col'), may hold values from -1.5 to 1.5
- w_out: bfloat16 [2, 768, 768], P(None, 'col', 'row'), may hold values from -1.75 to 1.75
- b_out: bfloat16 [2, 768], P(None, 'row'), may hold values from -1.5 to 1.5
- up_weight: bfloat16 [2, 768, 3072], P(None, 'row', 'col'), may hold values from -0.21875 to 0.21875
- up_bias: bfloat16 [2, 3072], P(None, 'col'), may hold values from -1.5 to 1.5
- down_weight: bfloat16 [2, 3072, 768], P(None, 'col', 'row'), may hold values from -0.109375 to 0.109375
- down_bias: bfloat16 [2, 768], P(None, 'row'), may hold values from -1.5 to 1.5
Outputs:
- result: bfloat16 [8, 256, 768], P('dp', None, 'row')
- tokens_grad: bfloat16 [8, 256, 768], P('dp', None, 'row')
- condition_grad: bfloat16 [8, 768], P('dp', 'col')
- w_ada_grad: float32 [2, 768, 6, 768], P(None, 'col', None, 'row')
- b_ada_grad: float32 [2, 6, 768], P(None, None, 'row')
- w_qkv_grad: float32 [2, 768, 3, 768], P(None, 'row', None, 'col')
- b_qv_grad: float32 [2, 2, 768], P(None, None, 'col')
- w_out_grad: float32 [2, 768, 768], P(None, 'col', 'row')
- b_out_grad: float32 [2, 768], P(None, 'row')
- w_up_grad: float32 [2, 768, 3072], P(None, 'row', 'col')
- b_up_grad: float32 [2, 3072], P(None, 'col')
- w_down_grad: float32 [2, 3072, 768], P(None, 'col', 'row')
- b_down_grad: float32 [2, 768], P(None, 'row')
The draws below stay inside these ranges and needn't reach their ends.
All inputs are finite; a program needn't handle non-finite values.
Results may differ from the reference program's by a relative error of at most 0.025.
Values may be sent and summed in bfloat16 or wider, within the bound.
A program may use at most 128 MiB of HBM per device.

```python
import jax
import jax.numpy as jnp
from jax import lax

D = 768
FF = 3072
HEAD = 64
SEQ = 256
LAYERS = 2
LAT_DEV = 2
BATCH = 8
N_DP = 4


def block_scale(key, dims, shards, low, largest):
    gain, own = 1.0, jax.random.fold_in(key, 6)
    for axis_at, blocks in shards:
        heights = jnp.exp(jax.random.uniform(jax.random.fold_in(own, axis_at), (blocks,), jnp.float32, low / len(shards), largest / len(shards)))
        gain = gain * jnp.repeat(heights, dims[axis_at] // blocks).reshape([-1 if axis == axis_at else 1 for axis in range(len(dims))])
    return gain


def bell_draw(key, shape, scale, limit, shards=(), held_as=jnp.bfloat16):
    factor_of = block_scale(key, shape, shards, -0.22, 0.18) if shards else 1.0
    array = jax.random.normal(key, shape, jnp.float32) * scale * factor_of
    return jnp.minimum(jnp.maximum(array, -limit), limit).astype(held_as)


def setup_inputs(seed: int = 0) -> dict:
    arg_keys = jax.random.split(jax.random.key(seed), 14)
    return {
        "tokens": bell_draw(arg_keys[0], (BATCH, SEQ, D), 1.0, 6.0, ((0, 4), (2, 2))),
        "condition": bell_draw(arg_keys[1], (BATCH, D), 1.0, 5.0, ((0, 4), (1, 4))),
        "cotangent": bell_draw(arg_keys[2], (BATCH, SEQ, D), 1.0, 6.0, ((0, 4), (2, 2))),
        "w_ada": bell_draw(arg_keys[3], (LAYERS, D, 6, D), D ** -0.5, 0.21875, ((1, 4), (3, 2))),
        "b_ada": bell_draw(arg_keys[4], (LAYERS, 6, D), 0.3, 1.5, ((2, 2),)),
        "w_qkv": bell_draw(arg_keys[5], (LAYERS, D, 3, D), D ** -0.5, 0.21875, ((1, 2), (3, 4))),
        "b_qv": bell_draw(arg_keys[6], (LAYERS, 2, D), 0.3, 1.5, ((2, 4),)),
        "w_out": bell_draw(arg_keys[7], (LAYERS, D, D), (D // 64) ** -0.5, 1.75, ((1, 4), (2, 2))),
        "b_out": bell_draw(arg_keys[8], (LAYERS, D), 0.3, 1.5, ((1, 2),)),
        "up_weight": bell_draw(arg_keys[9], (LAYERS, D, FF), D ** -0.5, 0.21875, ((1, 2), (2, 4))),
        "up_bias": bell_draw(arg_keys[10], (LAYERS, FF), 0.3, 1.5, ((1, 4),)),
        "down_weight": bell_draw(arg_keys[11], (LAYERS, FF, D), FF ** -0.5, 0.109375, ((1, 4), (2, 2))),
        "down_bias": bell_draw(arg_keys[12], (LAYERS, D), 0.3, 1.5, ((1, 2),)),
    }


@jax.custom_vjp
def low(v):
    return lax.optimization_barrier(v.astype(jnp.bfloat16)).astype(jnp.float32)

@jax.custom_vjp
def lowered_backward(v):
    return v

def low_keep(v):
    return (low(v), None)

def low_pass(kept, grad):
    return (grad,)

def back_keep(v):
    return (v, None)

def back_low(kept, grad):
    return (low(grad),)
low.defvjp(low_keep, low_pass)
lowered_backward.defvjp(back_keep, back_low)
EPSILON = 1e-06
FULL_PRECISION = lax.Precision.HIGHEST

def layer_norm(values):
    average = lax.optimization_barrier(jnp.mean(values, axis=-1, keepdims=True))
    spread = lax.optimization_barrier(jnp.mean(values * values, axis=-1, keepdims=True)) - average * average
    return (values - average) * lax.rsqrt(spread + EPSILON)

def gelu_tanh(values):
    return 0.5 * values * (1.0 + jnp.tanh(0.7978845608028654 * (values + 0.044715 * values * values * values)))

def one_layer(stream, cond_low, w_ada, b_ada, w_qkv, b_qv, w_out, b_out, up_weight, up_bias, down_weight, down_bias):
    latents = stream.shape[0]
    modulation = lowered_backward(jnp.einsum('lc,ckd->lkd', cond_low, w_ada, precision=FULL_PRECISION) + b_ada)
    shift_one, scale_one, gate_one, shift_two, scale_two, gate_two = [modulation[:, slot_index][:, None, :] for slot_index in range(6)]
    hidden_one = low(layer_norm(stream) * (1.0 + scale_one) + shift_one)
    bias_three = jnp.stack([b_qv[0], jnp.zeros_like(b_qv[0]), b_qv[1]])
    projected = jnp.einsum('lsd,dke->lske', hidden_one, w_qkv, precision=FULL_PRECISION) + bias_three
    projected = low(lowered_backward(projected))
    head_view = projected.reshape(latents, SEQ, 3, D // HEAD, HEAD)
    queries, key_rows, value_rows = (head_view[:, :, 0], head_view[:, :, 1], head_view[:, :, 2])
    scores = lowered_backward(jnp.einsum('lqhe,lkhe->lhqk', queries, key_rows, precision=FULL_PRECISION) * HEAD ** (-0.5))
    highest = lax.optimization_barrier(jnp.max(scores, axis=-1, keepdims=True))
    expos = jnp.exp(scores - highest)
    weights_soft = expos / lax.optimization_barrier(jnp.sum(expos, axis=-1, keepdims=True))
    head_mix = jnp.einsum('lhqk,lkhe->lqhe', low(weights_soft), value_rows, precision=FULL_PRECISION).reshape(latents, SEQ, D)
    head_mix = low(lowered_backward(head_mix))
    attention = lowered_backward(jnp.einsum('lsc,cd->lsd', head_mix, w_out, precision=FULL_PRECISION) + b_out)
    stream = stream + gate_one * attention
    second_hidden = low(layer_norm(stream) * (1.0 + scale_two) + shift_two)
    before_feed = lowered_backward(jnp.einsum('zha,aw->zhw', second_hidden, up_weight, precision=FULL_PRECISION) + up_bias)
    activated_hidden = low(gelu_tanh(before_feed))
    feed_output = lowered_backward(jnp.einsum('pqc,ct->pqt', activated_hidden, down_weight, precision=FULL_PRECISION) + down_bias)
    return stream + gate_two * feed_output

def reference(tokens, condition, cotangent, w_ada, b_ada, w_qkv, b_qv, w_out, b_out, up_weight, up_bias, down_weight, down_bias):
    params = tuple((one_array.astype(jnp.float32) for one_array in (w_ada, b_ada, w_qkv, b_qv, w_out, b_out, up_weight, up_bias, down_weight, down_bias)))

    def forward(weights_all, stream, cond_group):
        cond_low = low(cond_group * jax.nn.sigmoid(cond_group))
        for layer_position in range(LAYERS):
            stream = one_layer(stream, cond_low, *[one_array[layer_position] for one_array in weights_all])
        return stream

    def one_group(totals, batch_item):
        stream, cond_group, upstream = batch_item
        outcome, pull_back = jax.vjp(forward, params, stream, cond_group)
        layer_sums, stream_grad, cond_grad = pull_back(upstream)
        return (jax.tree.map(jnp.add, totals, layer_sums), (outcome, stream_grad, cond_grad))
    shaped = tokens.astype(jnp.float32).reshape(N_DP, LAT_DEV, SEQ, D)
    cond_groups = condition.astype(jnp.float32).reshape(N_DP, LAT_DEV, D)
    upstreams = cotangent.astype(jnp.float32).reshape(N_DP, LAT_DEV, SEQ, D)
    totals, (outcome, stream_grad, cond_grad) = lax.scan(one_group, jax.tree.map(jnp.zeros_like, params), (shaped, cond_groups, upstreams))
    return (outcome.reshape(BATCH, SEQ, D).astype(jnp.bfloat16), stream_grad.reshape(BATCH, SEQ, D).astype(jnp.bfloat16), cond_grad.reshape(BATCH, D).astype(jnp.bfloat16), totals[0], totals[1], totals[2], totals[3], totals[4], totals[5], totals[6], totals[7], totals[8], totals[9])
```

```python
import functools

import jax
import jax.numpy as jnp
from jax import lax
from jax.experimental import pallas as pl
from jax.experimental.pallas import tpu as pltpu
from jax.sharding import PartitionSpec as P

HEAD = 64
EPSILON = 1e-06
MESH = pl.DeviceIdType.MESH
F32 = jnp.float32
BF16 = jnp.bfloat16


def silu_plain(values):
    return values * jax.nn.sigmoid(values)


def dot(a, b, ca=1, cb=0):
    return lax.dot_general(a, b, (((ca,), (cb,)), ((), ())), preferred_element_type=F32)


def gelu_parts(u):
    inner = 0.7978845608028654 * (u + 0.044715 * u * u * u)
    t = jnp.tanh(inner)
    value = 0.5 * u * (1.0 + t)
    slope = 0.5 * (1.0 + t) + 0.5 * u * (1.0 - t * t) * 0.7978845608028654 * (
        1.0 + 3.0 * 0.044715 * u * u
    )
    return value, slope


def gelu_value(u):
    return 0.5 * u * (1.0 + jnp.tanh(0.7978845608028654 * (u + 0.044715 * u * u * u)))


def gelu_slope(u):
    return gelu_parts(u)[1]


def layer_norm(v):
    average = jnp.mean(v, axis=-1, keepdims=True)
    square = jnp.mean(v * v, axis=-1, keepdims=True)
    inverse = lax.rsqrt(square - average * average + EPSILON)
    return (v - average) * inverse, inverse


def norm_back(g, normed, inverse):
    first = jnp.mean(g, axis=-1, keepdims=True)
    second = jnp.mean(g * normed, axis=-1, keepdims=True)
    return inverse * (g - first - normed * second)


def col_sum(v):
    return jnp.sum(v, axis=0, keepdims=True)


def softmax_parts(q, k):
    scores = dot(q, k, 1, 1) * HEAD ** (-0.5)
    expos = jnp.exp(scores - jnp.max(scores, axis=-1, keepdims=True))
    return expos / jnp.sum(expos, axis=-1, keepdims=True)


def block_kernel(
    layers, n_row, n_col, tokens, cotangent, mod_part, w_qkv, w_out, w_up, w_down,
    b_qkv, b_out, b_up, b_down,
    result, tok_grad, g_qkv, g_out, g_up, g_down, small,
    wq, wo, wu, wd, tok, cot, modbuf, mod, ag, rs, rs_send, own_send, gat,
    proj, mix, attn, n1, i1, n2, i2, before, act, feed, stream,
    gq_s, go_s, gu_s, gd_s, gq_r, go_r, gu_r, gd_r, res_send, res_r,
    ph_send, ph_recv, w_local, w_send, w_recv, g_send, g_recv, p_send, p_recv, t_local, t_send, t_recv,
):
    r = lax.axis_index("row")
    c = lax.axis_index("col")
    group = n_row * n_col
    peers = []
    for k in range(1, group):
        idx = lax.rem(r * n_col + c + k, group)
        peers.append((k, idx // n_col, lax.rem(idx, n_col)))
    barrier = pltpu.get_barrier_semaphore()
    for _, pr, pc in peers:
        pl.semaphore_signal(barrier, inc=1, device_id={"row": pr, "col": pc}, device_id_type=MESH)
    pl.semaphore_wait(barrier, group - 1)
    other = n_row - 1 - r
    mate = {"row": other, "col": c}
    chunk = tokens.shape[1] // n_col
    full = tokens.shape[1]
    pending = []

    def remote(src, dst, ss, rsem, where):
        cp = pltpu.make_async_remote_copy(
            src_ref=src, dst_ref=dst, send_sem=ss, recv_sem=rsem, device_id=where, device_id_type=MESH
        )
        cp.start()
        pending.append(cp)
        return cp

    mod_copies = []
    for k, pr, pc in peers:
        mod_copies.append(
            remote(mod_part.at[pr], modbuf.at[r, c], p_send.at[0, k], p_recv.at[0, k], {"row": pr, "col": pc})
        )
    rows = pl.ds(pl.multiple_of(c * chunk, chunk), chunk)
    tok_copies = []
    for n, (src, dst) in enumerate(((tokens, tok), (cotangent, cot))):
        if n == 0:
            tok_copies.append(remote(src.at[other, rows], dst.at[r], t_send.at[n], t_recv.at[n], mate))
        here = pltpu.make_async_copy(src.at[r, rows], dst.at[r], t_local.at[n])
        here.start()
        tok_copies.append(here)
    weights = [(w_qkv, wq), (w_out, wo), (w_up, wu), (w_down, wd)]
    w_copies = {}
    for l in range(layers):
        for n, (src, dst) in enumerate(weights):
            s = l * 4 + n
            far = remote(src.at[l], dst.at[l, r], w_send.at[s], w_recv.at[s], mate)
            here = pltpu.make_async_copy(src.at[l], dst.at[l, r], w_local.at[s])
            here.start()
            w_copies[(l, n)] = (far, here)
    cot_far = remote(cotangent.at[other, rows], cot.at[r], t_send.at[1], t_recv.at[1], mate)

    def need(l, n):
        far, here = w_copies[(l, n)]
        far.wait_recv()
        here.wait()

    def gather_start(ph, value):
        ag[ph, c] = value
        out = []
        for k in range(1, n_col):
            where = {"row": r, "col": lax.rem(c + k, n_col)}
            out.append(remote(ag.at[ph, c], ag.at[ph, c], ph_send.at[2 * ph, k], ph_recv.at[2 * ph, k], where))
        return out

    def gather_end(ph, copies):
        for cp in copies:
            cp.wait_recv()
        return ag[ph].reshape(full, ag.shape[-1])

    def gathered(ph):
        return ag[ph].reshape(full, ag.shape[-1])

    def scatter_start(ph, parts):
        half = parts[0].shape[1]
        for j, part in enumerate(parts):
            rs_send[ph, :, :, j * half:(j + 1) * half] = part.astype(BF16).reshape(n_col, chunk, half)
        out = []
        for k in range(1, n_col):
            to = lax.rem(c + k, n_col)
            out.append(
                remote(
                    rs_send.at[ph, to], rs.at[ph, k - 1], ph_send.at[2 * ph + 1, k],
                    ph_recv.at[2 * ph + 1, k], {"row": r, "col": to},
                )
            )
        return out

    def scatter_end(ph, copies):
        total = rs_send[ph, c].astype(F32)
        for k, cp in enumerate(copies):
            cp.wait_recv()
            total = total + rs[ph, k].astype(F32)
        return total

    def modrow(l, slot):
        return mod[l * 6 + slot:l * 6 + slot + 1, :]

    width = n_row * tokens.shape[2]
    half = tokens.shape[2]
    heads_w = mix.shape[-1]
    n_heads = heads_w // HEAD

    def spread(ph, value, slot, buf_out):
        for j in range(n_row):
            res_send[slot, j] = value[:, j * half:(j + 1) * half]
        out = []
        for k, pr, pc in peers:
            out.append(
                remote(
                    res_send.at[slot, pr], res_r.at[slot, r, c], p_send.at[1 + slot, k],
                    p_recv.at[1 + slot, k], {"row": pr, "col": pc},
                )
            )
        res_r[slot, r, c] = res_send[slot, r]
        return out

    def spread_end(copies, slot, out_ref):
        for cp in copies:
            cp.wait_recv()
        out_ref[...] = res_r[slot]

    modbuf[r, c] = mod_part[r]
    for cp in mod_copies:
        cp.wait_recv()
    for j in range(n_row):
        total = modbuf[j, 0]
        for k in range(1, n_col):
            total = total + modbuf[j, k]
        mod[:, j * half:(j + 1) * half] = total
    tok_copies[0].wait_recv()
    tok_copies[1].wait()
    tok_copies[2].wait()
    x = jnp.concatenate([tok[j] for j in range(n_row)], axis=1).astype(F32)

    for l in range(layers):
        normed, inverse = layer_norm(x)
        n1[l] = normed
        i1[l] = inverse
        hidden = (normed * (1.0 + modrow(l, 1)) + modrow(l, 0)).astype(BF16)
        ph = 4 * l
        copies = gather_start(ph, hidden)
        need(l, 0)
        hid = gather_end(ph, copies)
        p = dot(hid[:, :half], wq[l, 0]) + dot(hid[:, half:], wq[l, 1])
        proj[l] = (p + b_qkv[l:l + 1, :]).astype(BF16)
        for h in range(n_heads):
            lo = h * HEAD
            q = proj[l, :, lo:lo + HEAD]
            kk = proj[l, :, heads_w + lo:heads_w + lo + HEAD]
            vv = proj[l, :, 2 * heads_w + lo:2 * heads_w + lo + HEAD]
            soft = softmax_parts(q, kk).astype(BF16)
            mix[l, :, lo:lo + HEAD] = dot(soft, vv).astype(BF16)
        need(l, 1)
        m = mix[l]
        copies = scatter_start(ph, [dot(m, wo[l, j]) for j in range(n_row)])
        attention = scatter_end(ph, copies) + b_out[l:l + 1, :]
        attn[l] = attention
        x = x + modrow(l, 2) * attention
        stream[l] = x
        normed, inverse = layer_norm(x)
        n2[l] = normed
        i2[l] = inverse
        hidden = (normed * (1.0 + modrow(l, 4)) + modrow(l, 3)).astype(BF16)
        ph = 4 * l + 1
        copies = gather_start(ph, hidden)
        need(l, 2)
        hid = gather_end(ph, copies)
        u = dot(hid[:, :half], wu[l, 0]) + dot(hid[:, half:], wu[l, 1]) + b_up[l:l + 1, :]
        before[l] = u
        act[l] = gelu_value(u).astype(BF16)
        need(l, 3)
        a = act[l]
        copies = scatter_start(ph, [dot(a, wd[l, j]) for j in range(n_row)])
        fo = scatter_end(ph, copies) + b_down[l:l + 1, :]
        feed[l] = fo
        x = x + modrow(l, 5) * fo
    res_copies = spread(0, x.astype(BF16), 0, result)
    cot_far.wait_recv()
    g = jnp.concatenate([cot[j] for j in range(n_row)], axis=1).astype(F32)

    grads = [(gq_s, gq_r, g_qkv), (go_s, go_r, g_out), (gu_s, gu_r, g_up), (gd_s, gd_r, g_down)]
    g_copies = []

    def grad_send(l, n):
        src, dst, out = grads[n]
        s = l * 4 + n
        cp = remote(src.at[l, other], dst.at[l], g_send.at[s], g_recv.at[s], mate)
        g_copies.append((l, n, cp))

    small[...] = jnp.zeros_like(small)
    for l in reversed(range(layers)):
        ph = 4 * l + 2
        gf = (g * modrow(l, 5)).astype(BF16)
        copies = gather_start(ph, gf)
        small[l * 6 + 5:l * 6 + 6, :] = col_sum(g * feed[l])
        small[12 + l:13 + l, :] = col_sum(gf.astype(F32))
        slope = gelu_slope(before[l])
        gf_all = gather_end(ph, copies)
        ga = dot(gf_all[:, :half], wd[l, 0], 1, 1) + dot(gf_all[:, half:], wd[l, 1], 1, 1)
        gb = (ga * slope).astype(BF16)
        copies = scatter_start(ph, [dot(gb, wu[l, j], 1, 1) for j in range(n_row)])
        a = act[l]
        for j in range(n_row):
            gd_s[l, j] = dot(a, gf_all[:, j * half:(j + 1) * half], 0, 0).astype(BF16)
        grad_send(l, 3)
        small[16 + l:17 + l, :] = col_sum(gb.astype(F32))
        hid2 = gathered(4 * l + 1)
        for j in range(n_row):
            gu_s[l, j] = dot(hid2[:, j * half:(j + 1) * half], gb, 0, 0).astype(BF16)
        grad_send(l, 2)
        gh = scatter_end(ph, copies)
        normed = n2[l]
        gm = g + norm_back(gh * (1.0 + modrow(l, 4)), normed, i2[l])
        gattn = (gm * modrow(l, 2)).astype(BF16)
        ph = 4 * l + 3
        copies = gather_start(ph, gattn)
        small[l * 6 + 4:l * 6 + 5, :] = col_sum(gh * normed)
        small[l * 6 + 3:l * 6 + 4, :] = col_sum(gh)
        small[l * 6 + 2:l * 6 + 3, :] = col_sum(gm * attn[l])
        small[14 + l:15 + l, :] = col_sum(gattn.astype(F32))
        ga_all = gather_end(ph, copies)
        gmix = (
            dot(ga_all[:, :half], wo[l, 0], 1, 1) + dot(ga_all[:, half:], wo[l, 1], 1, 1)
        ).astype(BF16)
        scale = HEAD ** (-0.5)
        for h in range(n_heads):
            lo = h * HEAD
            q = proj[l, :, lo:lo + HEAD]
            kk = proj[l, :, heads_w + lo:heads_w + lo + HEAD]
            vv = proj[l, :, 2 * heads_w + lo:2 * heads_w + lo + HEAD]
            gh_ = gmix[:, lo:lo + HEAD]
            soft = softmax_parts(q, kk)
            gs = dot(gh_, vv, 1, 1)
            gsc = (soft * (gs - jnp.sum(soft * gs, axis=-1, keepdims=True))).astype(BF16)
            gat[:, lo:lo + HEAD] = (dot(gsc, kk) * scale).astype(BF16)
            gat[:, heads_w + lo:heads_w + lo + HEAD] = (dot(gsc, q, 0, 0) * scale).astype(BF16)
            gat[:, 2 * heads_w + lo:2 * heads_w + lo + HEAD] = dot(soft.astype(BF16), gh_, 0, 0).astype(BF16)
        gp = gat[...]
        copies = scatter_start(ph, [dot(gp, wq[l, j], 1, 1) for j in range(n_row)])
        hid1 = gathered(4 * l)
        for j in range(n_row):
            gq_s[l, j] = dot(hid1[:, j * half:(j + 1) * half], gp, 0, 0).astype(BF16)
        grad_send(l, 0)
        m = mix[l]
        for j in range(n_row):
            go_s[l, j] = dot(m, ga_all[:, j * half:(j + 1) * half], 0, 0).astype(BF16)
        grad_send(l, 1)
        small[18 + l:19 + l, :gp.shape[1]] = col_sum(gp.astype(F32))
        gh = scatter_end(ph, copies)
        normed = n1[l]
        small[l * 6 + 1:l * 6 + 2, :] = col_sum(gh * normed)
        small[l * 6:l * 6 + 1, :] = col_sum(gh)
        g = gm + norm_back(gh * (1.0 + modrow(l, 1)), normed, i1[l])
    tg_copies = spread(1, g.astype(BF16), 1, tok_grad)
    for l, n, cp in g_copies:
        src, dst, out = grads[n]
        cp.wait_recv()
        out[l] = (src[l, r].astype(F32) + dst[l].astype(F32)).astype(BF16)
    spread_end(res_copies, 0, result)
    spread_end(tg_copies, 1, tok_grad)
    for cp in pending:
        cp.wait_send()


def run_blocks(n_row, n_col, tokens, cotangent, mod_part, w_qkv, w_out, w_up, w_down, b_qkv, b_out, b_up, b_down):
    layers, half, qkv_w = w_qkv.shape
    full = tokens.shape[1]
    chunk = full // n_col
    width = half * n_row
    head_w = w_out.shape[1]
    hid = w_up.shape[2]
    any_spec = pl.BlockSpec(memory_space=pl.ANY)
    vmem = pl.BlockSpec(memory_space=pltpu.VMEM)
    group = n_row * n_col
    out_shape = (
        jax.ShapeDtypeStruct((n_row, n_col, chunk, half), BF16),
        jax.ShapeDtypeStruct((n_row, n_col, chunk, half), BF16),
        jax.ShapeDtypeStruct((layers, half, qkv_w), BF16),
        jax.ShapeDtypeStruct((layers, head_w, half), BF16),
        jax.ShapeDtypeStruct((layers, half, hid), BF16),
        jax.ShapeDtypeStruct((layers, hid, half), BF16),
        jax.ShapeDtypeStruct((24, width), F32),
    )
    dma = pltpu.SemaphoreType.DMA
    v = pltpu.VMEM
    phases = 4 * layers
    scratch = [
        v((layers, n_row, half, qkv_w), BF16),
        v((layers, n_row, head_w, half), BF16),
        v((layers, n_row, half, hid), BF16),
        v((layers, n_row, hid, half), BF16),
        v((n_row, chunk, half), BF16),
        v((n_row, chunk, half), BF16),
        v((n_row, n_col) + mod_part.shape[1:], F32),
        v((mod_part.shape[1], width), F32),
        v((phases, n_col, chunk, width), BF16),
        v((phases, n_col - 1, chunk, width), BF16),
        v((phases, n_col, chunk, width), BF16),
        v((16, 128), BF16),
        v((full, qkv_w), BF16),
        v((layers, full, qkv_w), BF16),
        v((layers, full, head_w), BF16),
        v((layers, chunk, width), F32),
        v((layers, chunk, width), F32),
        v((layers, chunk, 1), F32),
        v((layers, chunk, width), F32),
        v((layers, chunk, 1), F32),
        v((layers, full, hid), F32),
        v((layers, full, hid), BF16),
        v((layers, chunk, width), F32),
        v((layers, chunk, width), F32),
        v((layers, n_row, half, qkv_w), BF16),
        v((layers, n_row, head_w, half), BF16),
        v((layers, n_row, half, hid), BF16),
        v((layers, n_row, hid, half), BF16),
        v((layers, half, qkv_w), BF16),
        v((layers, head_w, half), BF16),
        v((layers, half, hid), BF16),
        v((layers, hid, half), BF16),
        v((2, n_row, chunk, half), BF16),
        v((2, n_row, n_col, chunk, half), BF16),
        dma((2 * phases, n_col)),
        dma((2 * phases, n_col)),
        dma((4 * layers,)),
        dma((4 * layers,)),
        dma((4 * layers,)),
        dma((4 * layers,)),
        dma((4 * layers,)),
        dma((3, group)),
        dma((3, group)),
        dma((2,)),
        dma((2,)),
        dma((2,)),
    ]
    return pl.pallas_call(
        functools.partial(block_kernel, layers, n_row, n_col),
        out_shape=out_shape,
        in_specs=[any_spec, any_spec, vmem, any_spec, any_spec, any_spec, any_spec, vmem, vmem, vmem, vmem],
        out_specs=tuple([vmem] * 7),
        scratch_shapes=scratch,
        compiler_params=pltpu.CompilerParams(
            collective_id=0, has_side_effects=True, vmem_limit_bytes=58 * 1024 * 1024
        ),
        name="blocks",
    )(tokens, cotangent, mod_part, w_qkv, w_out, w_up, w_down, b_qkv, b_out, b_up, b_down)


def local(n_dp, n_row, n_col, tokens, condition, cotangent, w_ada, b_ada, w_qkv, b_qv, w_out, b_out,
          up_weight, up_bias, down_weight, down_bias):
    layers = w_ada.shape[0]
    half = tokens.shape[2]
    latents = tokens.shape[0]
    r = lax.axis_index("row")
    c = lax.axis_index("col")
    d = lax.axis_index("dp")
    cond_float = condition.astype(F32)
    cond_low = silu_plain(cond_float).astype(BF16)
    cond_all = lax.all_gather(cond_low, "dp", axis=0, tiled=True)
    part = jnp.einsum("lc,nckd->lnkd", cond_low, w_ada, preferred_element_type=F32)
    part = part + jnp.where(c == 0, b_ada.astype(F32), 0.0)[None]
    part = jnp.pad(part.reshape(latents, layers * 6, half), ((0, 0), (0, 4), (0, 0)))
    bq = b_qv.astype(F32)
    b_qkv = jnp.concatenate([bq[:, 0], jnp.zeros_like(bq[:, 0]), bq[:, 1]], axis=1)
    row_bias = lax.all_gather(jnp.stack([b_out, down_bias]), "row", axis=2, tiled=True).astype(F32)
    q_w = w_qkv.shape[3]
    res, tg, g_qkv, g_out, g_up, g_down, small = run_blocks(
        n_row, n_col, tokens, cotangent, part, w_qkv.reshape(layers, half, 3 * q_w), w_out, up_weight,
        down_weight, b_qkv, row_bias[0], up_bias.astype(F32), row_bias[1],
    )
    g_qkv, g_out, g_up, g_down = [
        t.astype(F32) for t in lax.psum((g_qkv, g_out, g_up, g_down), "dp")
    ]
    summed = lax.psum(small[:16], "col")
    table = jnp.concatenate([summed, small[16:20]], axis=0).astype(BF16)
    table = lax.all_gather(table, ("dp", "row"), axis=0)
    mine = lax.dynamic_slice_in_dim(table[:, :16], r * half, half, axis=2)
    gmod = mine[:, :12].reshape(-1, layers, 6, half)
    w_ada_grad = jnp.einsum("lc,lnkd->nckd", cond_all, gmod, preferred_element_type=F32)
    b_ada_grad = jnp.sum(gmod, axis=0, dtype=F32)
    own = lax.dynamic_slice_in_dim(gmod, d * latents, latents, axis=0)
    cond_term = lax.psum(jnp.einsum("lnkd,nckd->lc", own, w_ada, preferred_element_type=F32), "row")
    condition_grad = jax.vjp(silu_plain, cond_float)[1](cond_term)[0].astype(BF16)
    vec = jnp.sum(mine[:, 12:16], axis=0, dtype=F32)
    rest = jnp.sum(table[:, 16:20], axis=0, dtype=F32)
    b_qkv_g = rest[2:4, : 3 * q_w].reshape(layers, 3, q_w)
    return (
        res.reshape(tokens.shape),
        tg.reshape(tokens.shape),
        condition_grad,
        w_ada_grad,
        b_ada_grad,
        g_qkv.reshape(w_qkv.shape),
        jnp.stack([b_qkv_g[:, 0], b_qkv_g[:, 2]], axis=1),
        g_out,
        vec[2:4],
        g_up,
        rest[0:2],
        g_down,
        vec[0:2],
    )


def solution(mesh):
    in_specs = (
        P("dp", None, "row"),
        P("dp", "col"),
        P("dp", None, "row"),
        P(None, "col", None, "row"),
        P(None, None, "row"),
        P(None, "row", None, "col"),
        P(None, None, "col"),
        P(None, "col", "row"),
        P(None, "row"),
        P(None, "row", "col"),
        P(None, "col"),
        P(None, "col", "row"),
        P(None, "row"),
    )
    out_specs = (
        P("dp", None, "row"),
        P("dp", None, "row"),
        P("dp", "col"),
        P(None, "col", None, "row"),
        P(None, None, "row"),
        P(None, "row", None, "col"),
        P(None, None, "col"),
        P(None, "col", "row"),
        P(None, "row"),
        P(None, "row", "col"),
        P(None, "col"),
        P(None, "col", "row"),
        P(None, "row"),
    )
    sizes = [mesh.shape[a] for a in ("dp", "row", "col")]
    return jax.shard_map(
        functools.partial(local, *sizes), mesh=mesh, in_specs=in_specs, out_specs=out_specs, check_vma=False
    )
```

```python
import functools

import jax
import jax.numpy as jnp
from jax import lax
from jax.experimental import pallas as pl
from jax.experimental.pallas import tpu as pltpu
from jax.sharding import PartitionSpec as P

HEAD = 64
EPSILON = 1e-06
MESH = pl.DeviceIdType.MESH
F32 = jnp.float32
BF16 = jnp.bfloat16


def silu_plain(values):
    return values * jax.nn.sigmoid(values)


def dot(a, b, ca=1, cb=0):
    return lax.dot_general(a, b, (((ca,), (cb,)), ((), ())), preferred_element_type=F32)


def gelu_parts(u):
    inner = 0.7978845608028654 * (u + 0.044715 * u * u * u)
    t = jnp.tanh(inner)
    value = 0.5 * u * (1.0 + t)
    slope = 0.5 * (1.0 + t) + 0.5 * u * (1.0 - t * t) * 0.7978845608028654 * (
        1.0 + 3.0 * 0.044715 * u * u
    )
    return value, slope


def gelu_value(u):
    return 0.5 * u * (1.0 + jnp.tanh(0.7978845608028654 * (u + 0.044715 * u * u * u)))


def gelu_slope(u):
    return gelu_parts(u)[1]


def layer_norm(v):
    average = jnp.mean(v, axis=-1, keepdims=True)
    square = jnp.mean(v * v, axis=-1, keepdims=True)
    inverse = lax.rsqrt(square - average * average + EPSILON)
    return (v - average) * inverse, inverse


def norm_back(g, normed, inverse):
    first = jnp.mean(g, axis=-1, keepdims=True)
    second = jnp.mean(g * normed, axis=-1, keepdims=True)
    return inverse * (g - first - normed * second)


def col_sum(v):
    return jnp.sum(v, axis=0, keepdims=True)


def softmax_parts(q, k):
    scores = dot(q, k, 1, 1) * HEAD ** (-0.5)
    expos = jnp.exp(scores - jnp.max(scores, axis=-1, keepdims=True))
    return expos / jnp.sum(expos, axis=-1, keepdims=True)


def block_kernel(
    layers, n_dp, n_row, n_col, tokens, cotangent, mod_part, cond, w_qkv, w_out, w_up, w_down,
    b_qkv, b_out, b_up, b_down,
    result, tok_grad, g_qkv, g_out, g_up, g_down, table,
    small, col_r, tab_s,
    wq, wo, wu, wd, tok, cot, modbuf, mod, ag, rs, rs_send, own_send, gat,
    proj, mix, attn, n1, i1, n2, i2, before, act, feed, stream,
    gq_s, go_s, gu_s, gd_s, gq_r, go_r, gu_r, gd_r, zq, zo, zu, zd, yq, yo, yu, yd, xq, xo, xu, xd, res_send, res_r,
    ph_send, ph_recv, w_local, w_send, w_recv, g_send, g_recv, p_send, p_recv, t_local, t_send, t_recv,
    z_send, z_recv, c_send, c_recv, d_send, d_recv,
):
    r = lax.axis_index("row")
    c = lax.axis_index("col")
    d = lax.axis_index("dp")
    group = n_row * n_col
    tree = n_dp == 4
    line = n_dp * n_row
    peers = []
    for k in range(1, group):
        idx = lax.rem(r * n_col + c + k, group)
        peers.append((k, idx // n_col, lax.rem(idx, n_col)))
    barrier = pltpu.get_barrier_semaphore()
    for _, pr, pc in peers:
        pl.semaphore_signal(barrier, inc=1, device_id={"row": pr, "col": pc}, device_id_type=MESH)
    for k in range(1, n_dp):
        for j in range(n_row):
            where = {"dp": lax.rem(d + k, n_dp), "row": jnp.int32(j)}
            pl.semaphore_signal(barrier, inc=1, device_id=where, device_id_type=MESH)
    pl.semaphore_wait(barrier, group - 1 + n_row * (n_dp - 1))
    other = n_row - 1 - r
    mate = {"row": other, "col": c}
    chunk = tokens.shape[1] // n_col
    full = tokens.shape[1]
    pending = []

    def remote(src, dst, ss, rsem, where):
        cp = pltpu.make_async_remote_copy(
            src_ref=src, dst_ref=dst, send_sem=ss, recv_sem=rsem, device_id=where, device_id_type=MESH
        )
        cp.start()
        pending.append(cp)
        return cp

    mod_copies = []
    for k, pr, pc in peers:
        mod_copies.append(
            remote(mod_part.at[pr], modbuf.at[r, c], p_send.at[0, k], p_recv.at[0, k], {"row": pr, "col": pc})
        )
    rows = pl.ds(pl.multiple_of(c * chunk, chunk), chunk)
    tok_copies = []
    for n, (src, dst) in enumerate(((tokens, tok), (cotangent, cot))):
        if n == 0:
            tok_copies.append(remote(src.at[other, rows], dst.at[r], t_send.at[n], t_recv.at[n], mate))
        here = pltpu.make_async_copy(src.at[r, rows], dst.at[r], t_local.at[n])
        here.start()
        tok_copies.append(here)
    weights = [(w_qkv, wq), (w_out, wo), (w_up, wu), (w_down, wd)]
    w_copies = {}
    for l in range(layers):
        for n, (src, dst) in enumerate(weights):
            s = l * 4 + n
            far = remote(src.at[l], dst.at[l, r], w_send.at[s], w_recv.at[s], mate)
            here = pltpu.make_async_copy(src.at[l], dst.at[l, r], w_local.at[s])
            here.start()
            w_copies[(l, n)] = (far, here)
    cot_far = remote(cotangent.at[other, rows], cot.at[r], t_send.at[1], t_recv.at[1], mate)

    def need(l, n):
        far, here = w_copies[(l, n)]
        far.wait_recv()
        here.wait()

    def gather_start(ph, value):
        ag[ph, c] = value
        out = []
        for k in range(1, n_col):
            where = {"row": r, "col": lax.rem(c + k, n_col)}
            out.append(remote(ag.at[ph, c], ag.at[ph, c], ph_send.at[2 * ph, k], ph_recv.at[2 * ph, k], where))
        return out

    def gather_end(ph, copies):
        for cp in copies:
            cp.wait_recv()
        return ag[ph].reshape(full, ag.shape[-1])

    def gathered(ph):
        return ag[ph].reshape(full, ag.shape[-1])

    def scatter_start(ph, parts):
        half = parts[0].shape[1]
        for j, part in enumerate(parts):
            rs_send[ph, :, :, j * half:(j + 1) * half] = part.astype(BF16).reshape(n_col, chunk, half)
        out = []
        for k in range(1, n_col):
            to = lax.rem(c + k, n_col)
            out.append(
                remote(
                    rs_send.at[ph, to], rs.at[ph, k - 1], ph_send.at[2 * ph + 1, k],
                    ph_recv.at[2 * ph + 1, k], {"row": r, "col": to},
                )
            )
        return out

    def scatter_end(ph, copies):
        total = rs_send[ph, c].astype(F32)
        for k, cp in enumerate(copies):
            cp.wait_recv()
            total = total + rs[ph, k].astype(F32)
        return total

    def modrow(l, slot):
        return mod[l * 6 + slot:l * 6 + slot + 1, :]

    width = n_row * tokens.shape[2]
    half = tokens.shape[2]
    heads_w = mix.shape[-1]
    n_heads = heads_w // HEAD

    def spread(ph, value, slot, buf_out):
        for j in range(n_row):
            res_send[slot, j] = value[:, j * half:(j + 1) * half]
        out = []
        for k, pr, pc in peers:
            out.append(
                remote(
                    res_send.at[slot, pr], res_r.at[slot, r, c], p_send.at[1 + slot, k],
                    p_recv.at[1 + slot, k], {"row": pr, "col": pc},
                )
            )
        res_r[slot, r, c] = res_send[slot, r]
        return out

    def spread_end(copies, slot, out_ref):
        for cp in copies:
            cp.wait_recv()
        out_ref[...] = res_r[slot]

    modbuf[r, c] = mod_part[r]
    for cp in mod_copies:
        cp.wait_recv()
    for j in range(n_row):
        total = modbuf[j, 0]
        for k in range(1, n_col):
            total = total + modbuf[j, k]
        mod[:, j * half:(j + 1) * half] = total
    tok_copies[0].wait_recv()
    tok_copies[1].wait()
    tok_copies[2].wait()
    x = jnp.concatenate([tok[j] for j in range(n_row)], axis=1).astype(F32)

    for l in range(layers):
        normed, inverse = layer_norm(x)
        n1[l] = normed
        i1[l] = inverse
        hidden = (normed * (1.0 + modrow(l, 1)) + modrow(l, 0)).astype(BF16)
        ph = 4 * l
        copies = gather_start(ph, hidden)
        need(l, 0)
        hid = gather_end(ph, copies)
        p = dot(hid[:, :half], wq[l, 0]) + dot(hid[:, half:], wq[l, 1])
        proj[l] = (p + b_qkv[l:l + 1, :]).astype(BF16)
        for h in range(n_heads):
            lo = h * HEAD
            q = proj[l, :, lo:lo + HEAD]
            kk = proj[l, :, heads_w + lo:heads_w + lo + HEAD]
            vv = proj[l, :, 2 * heads_w + lo:2 * heads_w + lo + HEAD]
            soft = softmax_parts(q, kk).astype(BF16)
            mix[l, :, lo:lo + HEAD] = dot(soft, vv).astype(BF16)
        need(l, 1)
        m = mix[l]
        copies = scatter_start(ph, [dot(m, wo[l, j]) for j in range(n_row)])
        attention = scatter_end(ph, copies) + b_out[l:l + 1, :]
        attn[l] = attention
        x = x + modrow(l, 2) * attention
        stream[l] = x
        normed, inverse = layer_norm(x)
        n2[l] = normed
        i2[l] = inverse
        hidden = (normed * (1.0 + modrow(l, 4)) + modrow(l, 3)).astype(BF16)
        ph = 4 * l + 1
        copies = gather_start(ph, hidden)
        need(l, 2)
        hid = gather_end(ph, copies)
        u = dot(hid[:, :half], wu[l, 0]) + dot(hid[:, half:], wu[l, 1]) + b_up[l:l + 1, :]
        before[l] = u
        act[l] = gelu_value(u).astype(BF16)
        need(l, 3)
        a = act[l]
        copies = scatter_start(ph, [dot(a, wd[l, j]) for j in range(n_row)])
        fo = scatter_end(ph, copies) + b_down[l:l + 1, :]
        feed[l] = fo
        x = x + modrow(l, 5) * fo
    res_copies = spread(0, x.astype(BF16), 0, result)
    cot_far.wait_recv()
    g = jnp.concatenate([cot[j] for j in range(n_row)], axis=1).astype(F32)

    grads = [(gq_s, gq_r, g_qkv), (go_s, go_r, g_out), (gu_s, gu_r, g_up), (gd_s, gd_r, g_down)]
    g_copies = []

    def grad_send(l, n):
        src, dst, out = grads[n]
        s = l * 4 + n
        cp = remote(src.at[l, other], dst.at[l], g_send.at[s], g_recv.at[s], mate)
        g_copies.append((l, n, cp))

    near = [zq, zo, zu, zd]
    across = [yq, yo, yu, yd]
    sums = [xq, xo, xu, xd]
    inner = (d == 1) | (d == 2)
    leaf = jnp.logical_not(inner)
    pair = {"dp": d + 1 - 2 * lax.rem(d, 2)}
    facing = {"dp": 3 - d}

    def hop(l, n, step):
        s = l * 4 + n
        src, dst, where = (
            (sums[n], near[n], pair), (sums[n], across[n], facing), (near[n], near[n], pair)
        )[step]
        return pltpu.make_async_remote_copy(
            src_ref=src.at[l], dst_ref=dst.at[l], send_sem=z_send.at[s, step], recv_sem=z_recv.at[s, step],
            device_id=where, device_id_type=MESH,
        )

    def add_row(l, n, cp):
        src, dst, out = grads[n]
        cp.wait_recv()
        total = (src[l, r].astype(F32) + dst[l].astype(F32)).astype(BF16)
        if not tree:
            out[l] = total
            return
        sums[n][l] = total

        @pl.when(leaf)
        def _():
            hop(l, n, 0).start()

    def add_near(l, n, cp):
        @pl.when(inner)
        def _():
            hop(l, n, 0).wait_recv()
            sums[n][l] = (sums[n][l].astype(F32) + near[n][l].astype(F32)).astype(BF16)
            hop(l, n, 1).start()

    def add_across(l, n, cp):
        @pl.when(inner)
        def _():
            hop(l, n, 1).wait_recv()
            total = (sums[n][l].astype(F32) + across[n][l].astype(F32)).astype(BF16)
            near[n][l] = total
            hop(l, n, 2).start()
            grads[n][2][l] = total

    def finish(l, n, cp):
        @pl.when(leaf)
        def _():
            hop(l, n, 2).wait_recv()
            grads[n][2][l] = near[n][l]
            hop(l, n, 0).wait_send()

        @pl.when(inner)
        def _():
            hop(l, n, 1).wait_send()
            hop(l, n, 2).wait_send()

    stages = [add_row, add_near, add_across, finish] if tree else [add_row]
    queue = []

    def advance():
        while len(queue) < len(g_copies):
            queue.append(0)
        moves = []
        for i, (l, n, cp) in enumerate(g_copies):
            if queue[i] < len(stages):
                moves.append((stages[queue[i]], l, n, cp))
                queue[i] += 1
        for f, l, n, cp in moves:
            f(l, n, cp)
        return len(moves)

    small[...] = jnp.zeros_like(small)
    for l in reversed(range(layers)):
        ph = 4 * l + 2
        gf = (g * modrow(l, 5)).astype(BF16)
        copies = gather_start(ph, gf)
        small[l * 6 + 5:l * 6 + 6, :] = col_sum(g * feed[l])
        small[12 + l:13 + l, :] = col_sum(gf.astype(F32))
        slope = gelu_slope(before[l])
        advance()
        gf_all = gather_end(ph, copies)
        ga = dot(gf_all[:, :half], wd[l, 0], 1, 1) + dot(gf_all[:, half:], wd[l, 1], 1, 1)
        gb = (ga * slope).astype(BF16)
        copies = scatter_start(ph, [dot(gb, wu[l, j], 1, 1) for j in range(n_row)])
        a = act[l]
        for j in range(n_row):
            gd_s[l, j] = dot(a, gf_all[:, j * half:(j + 1) * half], 0, 0).astype(BF16)
        grad_send(l, 3)
        small[16 + l:17 + l, :] = col_sum(gb.astype(F32))
        hid2 = gathered(4 * l + 1)
        for j in range(n_row):
            gu_s[l, j] = dot(hid2[:, j * half:(j + 1) * half], gb, 0, 0).astype(BF16)
        grad_send(l, 2)
        gh = scatter_end(ph, copies)
        normed = n2[l]
        gm = g + norm_back(gh * (1.0 + modrow(l, 4)), normed, i2[l])
        gattn = (gm * modrow(l, 2)).astype(BF16)
        ph = 4 * l + 3
        copies = gather_start(ph, gattn)
        small[l * 6 + 4:l * 6 + 5, :] = col_sum(gh * normed)
        small[l * 6 + 3:l * 6 + 4, :] = col_sum(gh)
        small[l * 6 + 2:l * 6 + 3, :] = col_sum(gm * attn[l])
        small[14 + l:15 + l, :] = col_sum(gattn.astype(F32))
        ga_all = gather_end(ph, copies)
        gmix = (
            dot(ga_all[:, :half], wo[l, 0], 1, 1) + dot(ga_all[:, half:], wo[l, 1], 1, 1)
        ).astype(BF16)
        scale = HEAD ** (-0.5)
        for h in range(n_heads):
            lo = h * HEAD
            q = proj[l, :, lo:lo + HEAD]
            kk = proj[l, :, heads_w + lo:heads_w + lo + HEAD]
            vv = proj[l, :, 2 * heads_w + lo:2 * heads_w + lo + HEAD]
            gh_ = gmix[:, lo:lo + HEAD]
            soft = softmax_parts(q, kk)
            gs = dot(gh_, vv, 1, 1)
            gsc = (soft * (gs - jnp.sum(soft * gs, axis=-1, keepdims=True))).astype(BF16)
            gat[:, lo:lo + HEAD] = (dot(gsc, kk) * scale).astype(BF16)
            gat[:, heads_w + lo:heads_w + lo + HEAD] = (dot(gsc, q, 0, 0) * scale).astype(BF16)
            gat[:, 2 * heads_w + lo:2 * heads_w + lo + HEAD] = dot(soft.astype(BF16), gh_, 0, 0).astype(BF16)
        gp = gat[...]
        copies = scatter_start(ph, [dot(gp, wq[l, j], 1, 1) for j in range(n_row)])
        advance()
        hid1 = gathered(4 * l)
        for j in range(n_row):
            gq_s[l, j] = dot(hid1[:, j * half:(j + 1) * half], gp, 0, 0).astype(BF16)
        grad_send(l, 0)
        m = mix[l]
        for j in range(n_row):
            go_s[l, j] = dot(m, ga_all[:, j * half:(j + 1) * half], 0, 0).astype(BF16)
        grad_send(l, 1)
        small[18 + l:19 + l, :gp.shape[1]] = col_sum(gp.astype(F32))
        gh = scatter_end(ph, copies)
        normed = n1[l]
        small[l * 6 + 1:l * 6 + 2, :] = col_sum(gh * normed)
        small[l * 6:l * 6 + 1, :] = col_sum(gh)
        g = gm + norm_back(gh * (1.0 + modrow(l, 1)), normed, i1[l])
    tg_copies = spread(1, g.astype(BF16), 1, tok_grad)
    out = []
    for k in range(1, n_col):
        where = {"row": r, "col": lax.rem(c + k, n_col)}
        out.append(remote(small.at[:16], col_r.at[k - 1], c_send.at[k], c_recv.at[k], where))
    advance()
    total = small[:16]
    for k, cp in enumerate(out):
        cp.wait_recv()
        total = total + col_r[k]
    low = jnp.concatenate([small[16:24], cond[r]], axis=0)
    tab_s[...] = jnp.concatenate([total, low], axis=0).astype(BF16)
    me = d * n_row + r
    out = []
    for k in range(1, line):
        to = lax.rem(me + k, line)
        where = {"dp": to // n_row, "row": lax.rem(to, n_row)}
        out.append(remote(tab_s, table.at[me], d_send.at[k], d_recv.at[k], where))
    table[me] = tab_s[...]
    advance()
    for cp in out:
        cp.wait_recv()
    while advance():
        pass
    spread_end(res_copies, 0, result)
    spread_end(tg_copies, 1, tok_grad)
    for cp in pending:
        cp.wait_send()


def run_blocks(n_dp, n_row, n_col, tokens, cotangent, mod_part, cond, w_qkv, w_out, w_up, w_down, b_qkv, b_out, b_up, b_down):
    layers, half, qkv_w = w_qkv.shape
    full = tokens.shape[1]
    chunk = full // n_col
    width = half * n_row
    head_w = w_out.shape[1]
    hid = w_up.shape[2]
    any_spec = pl.BlockSpec(memory_space=pl.ANY)
    vmem = pl.BlockSpec(memory_space=pltpu.VMEM)
    group = n_row * n_col
    out_shape = (
        jax.ShapeDtypeStruct((n_row, n_col, chunk, half), BF16),
        jax.ShapeDtypeStruct((n_row, n_col, chunk, half), BF16),
        jax.ShapeDtypeStruct((layers, half, qkv_w), BF16),
        jax.ShapeDtypeStruct((layers, head_w, half), BF16),
        jax.ShapeDtypeStruct((layers, half, hid), BF16),
        jax.ShapeDtypeStruct((layers, hid, half), BF16),
        jax.ShapeDtypeStruct((n_dp * n_row, 32, width), BF16),
    )
    dma = pltpu.SemaphoreType.DMA
    v = pltpu.VMEM
    phases = 4 * layers
    grads = [(layers, half, qkv_w), (layers, head_w, half), (layers, half, hid), (layers, hid, half)]
    scratch = [
        v((24, width), F32),
        v((n_col - 1, 16, width), F32),
        v((32, width), BF16),
        v((layers, n_row, half, qkv_w), BF16),
        v((layers, n_row, head_w, half), BF16),
        v((layers, n_row, half, hid), BF16),
        v((layers, n_row, hid, half), BF16),
        v((n_row, chunk, half), BF16),
        v((n_row, chunk, half), BF16),
        v((n_row, n_col) + mod_part.shape[1:], F32),
        v((mod_part.shape[1], width), F32),
        v((phases, n_col, chunk, width), BF16),
        v((phases, n_col - 1, chunk, width), BF16),
        v((phases, n_col, chunk, width), BF16),
        v((16, 128), BF16),
        v((full, qkv_w), BF16),
        v((layers, full, qkv_w), BF16),
        v((layers, full, head_w), BF16),
        v((layers, chunk, width), F32),
        v((layers, chunk, width), F32),
        v((layers, chunk, 1), F32),
        v((layers, chunk, width), F32),
        v((layers, chunk, 1), F32),
        v((layers, full, hid), F32),
        v((layers, full, hid), BF16),
        v((layers, chunk, width), F32),
        v((layers, chunk, width), F32),
        v((layers, n_row, half, qkv_w), BF16),
        v((layers, n_row, head_w, half), BF16),
        v((layers, n_row, half, hid), BF16),
        v((layers, n_row, hid, half), BF16),
        v((layers, half, qkv_w), BF16),
        v((layers, head_w, half), BF16),
        v((layers, half, hid), BF16),
        v((layers, hid, half), BF16),
        *[v(g, BF16) for g in grads * 3],
        v((2, n_row, chunk, half), BF16),
        v((2, n_row, n_col, chunk, half), BF16),
        dma((2 * phases, n_col)),
        dma((2 * phases, n_col)),
        dma((4 * layers,)),
        dma((4 * layers,)),
        dma((4 * layers,)),
        dma((4 * layers,)),
        dma((4 * layers,)),
        dma((3, group)),
        dma((3, group)),
        dma((2,)),
        dma((2,)),
        dma((2,)),
        dma((4 * layers, 3)),
        dma((4 * layers, 3)),
        dma((n_col,)),
        dma((n_col,)),
        dma((n_dp * n_row,)),
        dma((n_dp * n_row,)),
    ]
    return pl.pallas_call(
        functools.partial(block_kernel, layers, n_dp, n_row, n_col),
        out_shape=out_shape,
        in_specs=[any_spec, any_spec, vmem, vmem, any_spec, any_spec, any_spec, any_spec, vmem, vmem, vmem, vmem],
        out_specs=tuple([vmem] * 7),
        scratch_shapes=scratch,
        compiler_params=pltpu.CompilerParams(
            collective_id=0, has_side_effects=True, vmem_limit_bytes=58 * 1024 * 1024
        ),
        name="blocks",
    )(tokens, cotangent, mod_part, cond, w_qkv, w_out, w_up, w_down, b_qkv, b_out, b_up, b_down)


def local(n_dp, n_row, n_col, tokens, condition, cotangent, w_ada, b_ada, w_qkv, b_qv, w_out, b_out,
          up_weight, up_bias, down_weight, down_bias):
    layers = w_ada.shape[0]
    half = tokens.shape[2]
    latents = tokens.shape[0]
    r = lax.axis_index("row")
    c = lax.axis_index("col")
    d = lax.axis_index("dp")
    cond_float = condition.astype(F32)
    cond_low = silu_plain(cond_float).astype(BF16)
    part = jnp.einsum("lc,nckd->lnkd", cond_low, w_ada, preferred_element_type=F32)
    part = part + jnp.where(c == 0, b_ada.astype(F32), 0.0)[None]
    part = jnp.pad(part.reshape(latents, layers * 6, half), ((0, 0), (0, 4), (0, 0)))
    cond_rows = jnp.pad(
        cond_low.astype(F32)[:, None], ((0, 0), (0, 7), (0, n_row * half - condition.shape[1]))
    )
    bq = b_qv.astype(F32)
    b_qkv = jnp.concatenate([bq[:, 0], jnp.zeros_like(bq[:, 0]), bq[:, 1]], axis=1)
    row_bias = lax.all_gather(jnp.stack([b_out, down_bias]), "row", axis=2, tiled=True).astype(F32)
    q_w = w_qkv.shape[3]
    res, tg, g_qkv, g_out, g_up, g_down, table = run_blocks(
        n_dp, n_row, n_col, tokens, cotangent, part, cond_rows, w_qkv.reshape(layers, half, 3 * q_w), w_out, up_weight,
        down_weight, b_qkv, row_bias[0], up_bias.astype(F32), row_bias[1],
    )
    sums = (g_qkv, g_out, g_up, g_down)
    if n_dp != 4:
        sums = lax.psum(sums, "dp")
    g_qkv, g_out, g_up, g_down = [t.astype(F32) for t in sums]
    cond_all = table[:, 24, : cond_low.shape[1]]
    mine = lax.dynamic_slice_in_dim(table[:, :16], r * half, half, axis=2)
    gmod = mine[:, :12].reshape(-1, layers, 6, half)
    w_ada_grad = jnp.einsum("lc,lnkd->nckd", cond_all, gmod, preferred_element_type=F32)
    b_ada_grad = jnp.sum(gmod, axis=0, dtype=F32)
    own = lax.dynamic_slice_in_dim(gmod, d * latents, latents, axis=0)
    cond_term = lax.psum(jnp.einsum("lnkd,nckd->lc", own, w_ada, preferred_element_type=F32), "row")
    condition_grad = jax.vjp(silu_plain, cond_float)[1](cond_term)[0].astype(BF16)
    vec = jnp.sum(mine[:, 12:16], axis=0, dtype=F32)
    rest = jnp.sum(table[:, 16:20], axis=0, dtype=F32)
    b_qkv_g = rest[2:4, : 3 * q_w].reshape(layers, 3, q_w)
    return (
        res.reshape(tokens.shape),
        tg.reshape(tokens.shape),
        condition_grad,
        w_ada_grad,
        b_ada_grad,
        g_qkv.reshape(w_qkv.shape),
        jnp.stack([b_qkv_g[:, 0], b_qkv_g[:, 2]], axis=1),
        g_out,
        vec[2:4],
        g_up,
        rest[0:2],
        g_down,
        vec[0:2],
    )


def solution(mesh):
    in_specs = (
        P("dp", None, "row"),
        P("dp", "col"),
        P("dp", None, "row"),
        P(None, "col", None, "row"),
        P(None, None, "row"),
        P(None, "row", None, "col"),
        P(None, None, "col"),
        P(None, "col", "row"),
        P(None, "row"),
        P(None, "row", "col"),
        P(None, "col"),
        P(None, "col", "row"),
        P(None, "row"),
    )
    out_specs = (
        P("dp", None, "row"),
        P("dp", None, "row"),
        P("dp", "col"),
        P(None, "col", None, "row"),
        P(None, None, "row"),
        P(None, "row", None, "col"),
        P(None, None, "col"),
        P(None, "col", "row"),
        P(None, "row"),
        P(None, "row", "col"),
        P(None, "col"),
        P(None, "col", "row"),
        P(None, "row"),
    )
    sizes = [mesh.shape[a] for a in ("dp", "row", "col")]
    return jax.shard_map(
        functools.partial(local, *sizes), mesh=mesh, in_specs=in_specs, out_specs=out_specs, check_vma=False
    )
```

```python
import functools

import jax
import jax.numpy as jnp
from jax import lax
from jax.experimental import pallas as pl
from jax.experimental.pallas import tpu as pltpu
from jax.sharding import PartitionSpec as P

HEAD = 64
EPSILON = 1e-06
MESH = pl.DeviceIdType.MESH
F32 = jnp.float32
BF16 = jnp.bfloat16


def silu_plain(values):
    return values * jax.nn.sigmoid(values)


def dot(a, b, ca=1, cb=0):
    return lax.dot_general(a, b, (((ca,), (cb,)), ((), ())), preferred_element_type=F32)


def gelu_parts(u):
    inner = 0.7978845608028654 * (u + 0.044715 * u * u * u)
    t = jnp.tanh(inner)
    value = 0.5 * u * (1.0 + t)
    slope = 0.5 * (1.0 + t) + 0.5 * u * (1.0 - t * t) * 0.7978845608028654 * (
        1.0 + 3.0 * 0.044715 * u * u
    )
    return value, slope


def gelu_value(u):
    return 0.5 * u * (1.0 + jnp.tanh(0.7978845608028654 * (u + 0.044715 * u * u * u)))


def gelu_slope(u):
    return gelu_parts(u)[1]


def layer_norm(v):
    average = jnp.mean(v, axis=-1, keepdims=True)
    square = jnp.mean(v * v, axis=-1, keepdims=True)
    inverse = lax.rsqrt(square - average * average + EPSILON)
    return (v - average) * inverse, inverse


def norm_back(g, normed, inverse):
    first = jnp.mean(g, axis=-1, keepdims=True)
    second = jnp.mean(g * normed, axis=-1, keepdims=True)
    return inverse * (g - first - normed * second)


def col_sum(v):
    return jnp.sum(v, axis=0, keepdims=True)


def softmax_parts(q, k):
    scores = dot(q, k, 1, 1) * HEAD ** (-0.5)
    expos = jnp.exp(scores - jnp.max(scores, axis=-1, keepdims=True))
    return expos / jnp.sum(expos, axis=-1, keepdims=True)


def block_kernel(
    layers, n_dp, n_row, n_col, tokens, cotangent, mod_part, cond, w_qkv, w_out, w_up, w_down,
    b_qkv, b_up,
    result, tok_grad, g_qkv, g_out, g_up, g_down, table,
    small, col_r, tab_s,
    wq, wo, wu, wd, tok, cot, modbuf, mod, ag, rs, rs_send, own_send, gat,
    proj, mix, attn, n1, i1, n2, i2, before, act, feed, stream,
    gq_s, go_s, gu_s, gd_s, gq_r, go_r, gu_r, gd_r, zq, zo, zu, zd, yq, yo, yu, yd, xq, xo, xu, xd, res_send, res_r,
    ph_send, ph_recv, w_local, w_send, w_recv, g_send, g_recv, p_send, p_recv, t_local, t_send, t_recv,
    z_send, z_recv, c_send, c_recv, d_send, d_recv,
):
    r = lax.axis_index("row")
    c = lax.axis_index("col")
    d = lax.axis_index("dp")
    group = n_row * n_col
    tree = n_dp == 4
    line = n_dp * n_row
    peers = []
    for k in range(1, group):
        idx = lax.rem(r * n_col + c + k, group)
        peers.append((k, idx // n_col, lax.rem(idx, n_col)))
    barrier = pltpu.get_barrier_semaphore()
    for _, pr, pc in peers:
        pl.semaphore_signal(barrier, inc=1, device_id={"row": pr, "col": pc}, device_id_type=MESH)
    for k in range(1, n_dp):
        for j in range(n_row):
            where = {"dp": lax.rem(d + k, n_dp), "row": jnp.int32(j)}
            pl.semaphore_signal(barrier, inc=1, device_id=where, device_id_type=MESH)
    pl.semaphore_wait(barrier, group - 1 + n_row * (n_dp - 1))
    other = n_row - 1 - r
    mate = {"row": other, "col": c}
    chunk = tokens.shape[1] // n_col
    full = tokens.shape[1]
    pending = []

    def remote(src, dst, ss, rsem, where):
        cp = pltpu.make_async_remote_copy(
            src_ref=src, dst_ref=dst, send_sem=ss, recv_sem=rsem, device_id=where, device_id_type=MESH
        )
        cp.start()
        pending.append(cp)
        return cp

    mod_copies = []
    for k, pr, pc in peers:
        mod_copies.append(
            remote(mod_part.at[pr], modbuf.at[r, c], p_send.at[0, k], p_recv.at[0, k], {"row": pr, "col": pc})
        )
    rows = pl.ds(pl.multiple_of(c * chunk, chunk), chunk)
    tok_copies = []
    for n, (src, dst) in enumerate(((tokens, tok), (cotangent, cot))):
        if n == 0:
            tok_copies.append(remote(src.at[other, rows], dst.at[r], t_send.at[n], t_recv.at[n], mate))
        here = pltpu.make_async_copy(src.at[r, rows], dst.at[r], t_local.at[n])
        here.start()
        tok_copies.append(here)
    weights = [(w_qkv, wq), (w_out, wo), (w_up, wu), (w_down, wd)]
    w_copies = {}
    for l in range(layers):
        for n, (src, dst) in enumerate(weights):
            s = l * 4 + n
            far = remote(src.at[l], dst.at[l, r], w_send.at[s], w_recv.at[s], mate)
            here = pltpu.make_async_copy(src.at[l], dst.at[l, r], w_local.at[s])
            here.start()
            w_copies[(l, n)] = (far, here)
    cot_far = remote(cotangent.at[other, rows], cot.at[r], t_send.at[1], t_recv.at[1], mate)

    def need(l, n):
        far, here = w_copies[(l, n)]
        far.wait_recv()
        here.wait()

    def gather_start(ph, value):
        ag[ph, c] = value
        out = []
        for k in range(1, n_col):
            where = {"row": r, "col": lax.rem(c + k, n_col)}
            out.append(remote(ag.at[ph, c], ag.at[ph, c], ph_send.at[2 * ph, k], ph_recv.at[2 * ph, k], where))
        return out

    def gather_end(ph, copies):
        for cp in copies:
            cp.wait_recv()
        return ag[ph].reshape(full, ag.shape[-1])

    def gathered(ph):
        return ag[ph].reshape(full, ag.shape[-1])

    def scatter_start(ph, parts):
        half = parts[0].shape[1]
        for j, part in enumerate(parts):
            rs_send[ph, :, :, j * half:(j + 1) * half] = part.astype(BF16).reshape(n_col, chunk, half)
        out = []
        for k in range(1, n_col):
            to = lax.rem(c + k, n_col)
            out.append(
                remote(
                    rs_send.at[ph, to], rs.at[ph, k - 1], ph_send.at[2 * ph + 1, k],
                    ph_recv.at[2 * ph + 1, k], {"row": r, "col": to},
                )
            )
        return out

    def scatter_end(ph, copies):
        total = rs_send[ph, c].astype(F32)
        for k, cp in enumerate(copies):
            cp.wait_recv()
            total = total + rs[ph, k].astype(F32)
        return total

    def modrow(l, slot):
        return mod[l * 6 + slot:l * 6 + slot + 1, :]

    width = n_row * tokens.shape[2]
    half = tokens.shape[2]
    heads_w = mix.shape[-1]
    n_heads = heads_w // HEAD

    def spread(ph, value, slot, buf_out):
        for j in range(n_row):
            res_send[slot, j] = value[:, j * half:(j + 1) * half]
        out = []
        for k, pr, pc in peers:
            out.append(
                remote(
                    res_send.at[slot, pr], res_r.at[slot, r, c], p_send.at[1 + slot, k],
                    p_recv.at[1 + slot, k], {"row": pr, "col": pc},
                )
            )
        res_r[slot, r, c] = res_send[slot, r]
        return out

    def spread_end(copies, slot, out_ref):
        for cp in copies:
            cp.wait_recv()
        out_ref[...] = res_r[slot]

    modbuf[r, c] = mod_part[r]
    for cp in mod_copies:
        cp.wait_recv()
    for j in range(n_row):
        total = modbuf[j, 0]
        for k in range(1, n_col):
            total = total + modbuf[j, k]
        mod[:, j * half:(j + 1) * half] = total
    tok_copies[0].wait_recv()
    tok_copies[1].wait()
    tok_copies[2].wait()
    x = jnp.concatenate([tok[j] for j in range(n_row)], axis=1).astype(F32)

    for l in range(layers):
        normed, inverse = layer_norm(x)
        n1[l] = normed
        i1[l] = inverse
        hidden = (normed * (1.0 + modrow(l, 1)) + modrow(l, 0)).astype(BF16)
        ph = 4 * l
        copies = gather_start(ph, hidden)
        need(l, 0)
        hid = gather_end(ph, copies)
        p = dot(hid[:, :half], wq[l, 0]) + dot(hid[:, half:], wq[l, 1])
        proj[l] = (p + b_qkv[l:l + 1, :]).astype(BF16)
        for h in range(n_heads):
            lo = h * HEAD
            q = proj[l, :, lo:lo + HEAD]
            kk = proj[l, :, heads_w + lo:heads_w + lo + HEAD]
            vv = proj[l, :, 2 * heads_w + lo:2 * heads_w + lo + HEAD]
            soft = softmax_parts(q, kk).astype(BF16)
            mix[l, :, lo:lo + HEAD] = dot(soft, vv).astype(BF16)
        need(l, 1)
        m = mix[l]
        copies = scatter_start(ph, [dot(m, wo[l, j]) for j in range(n_row)])
        attention = scatter_end(ph, copies) + mod[12 + l:13 + l, :]
        attn[l] = attention
        x = x + modrow(l, 2) * attention
        stream[l] = x
        normed, inverse = layer_norm(x)
        n2[l] = normed
        i2[l] = inverse
        hidden = (normed * (1.0 + modrow(l, 4)) + modrow(l, 3)).astype(BF16)
        ph = 4 * l + 1
        copies = gather_start(ph, hidden)
        need(l, 2)
        hid = gather_end(ph, copies)
        u = dot(hid[:, :half], wu[l, 0]) + dot(hid[:, half:], wu[l, 1]) + b_up[l:l + 1, :]
        before[l] = u
        act[l] = gelu_value(u).astype(BF16)
        need(l, 3)
        a = act[l]
        copies = scatter_start(ph, [dot(a, wd[l, j]) for j in range(n_row)])
        fo = scatter_end(ph, copies) + mod[12 + layers + l:13 + layers + l, :]
        feed[l] = fo
        x = x + modrow(l, 5) * fo
    res_copies = spread(0, x.astype(BF16), 0, result)
    cot_far.wait_recv()
    g = jnp.concatenate([cot[j] for j in range(n_row)], axis=1).astype(F32)

    grads = [(gq_s, gq_r, g_qkv), (go_s, go_r, g_out), (gu_s, gu_r, g_up), (gd_s, gd_r, g_down)]
    g_copies = []

    def span(n, p):
        size = grads[n][1].shape[1] // 2
        return pl.ds(p * size, size)

    def grad_send(l, n):
        src, dst, out = grads[n]
        for p in range(2):
            s = (l * 4 + n) * 2 + p
            cp = remote(src.at[l, other, span(n, p)], dst.at[l, span(n, p)], g_send.at[s], g_recv.at[s], mate)
            g_copies.append((l, (n, p), cp))

    near = [zq, zo, zu, zd]
    across = [yq, yo, yu, yd]
    sums = [xq, xo, xu, xd]
    inner = (d == 1) | (d == 2)
    leaf = jnp.logical_not(inner)
    pair = {"dp": d + 1 - 2 * lax.rem(d, 2)}
    facing = {"dp": 3 - d}

    def hop(l, item, step):
        n, p = item
        s = (l * 4 + n) * 2 + p
        src, dst, where = (
            (sums[n], near[n], pair), (sums[n], across[n], facing), (near[n], near[n], pair)
        )[step]
        return pltpu.make_async_remote_copy(
            src_ref=src.at[l, span(n, p)], dst_ref=dst.at[l, span(n, p)], send_sem=z_send.at[s, step], recv_sem=z_recv.at[s, step],
            device_id=where, device_id_type=MESH,
        )

    def add_row(l, item, cp):
        n, p = item
        at = span(n, p)
        src, dst, out = grads[n]
        cp.wait_recv()
        total = (src[l, r, at].astype(F32) + dst[l, at].astype(F32)).astype(BF16)
        if not tree:
            out[l, at] = total
            return
        sums[n][l, at] = total

        @pl.when(leaf)
        def _():
            hop(l, item, 0).start()

    def add_near(l, item, cp):
        n, p = item
        at = span(n, p)

        @pl.when(inner)
        def _():
            hop(l, item, 0).wait_recv()
            sums[n][l, at] = (sums[n][l, at].astype(F32) + near[n][l, at].astype(F32)).astype(BF16)
            hop(l, item, 1).start()

    def add_across(l, item, cp):
        n, p = item
        at = span(n, p)

        @pl.when(inner)
        def _():
            hop(l, item, 1).wait_recv()
            total = (sums[n][l, at].astype(F32) + across[n][l, at].astype(F32)).astype(BF16)
            near[n][l, at] = total
            hop(l, item, 2).start()
            grads[n][2][l, at] = total

    def finish(l, item, cp):
        n, p = item
        at = span(n, p)

        @pl.when(leaf)
        def _():
            hop(l, item, 2).wait_recv()
            grads[n][2][l, at] = near[n][l, at]
            hop(l, item, 0).wait_send()

        @pl.when(inner)
        def _():
            hop(l, item, 1).wait_send()
            hop(l, item, 2).wait_send()

    stages = [add_row, add_near, add_across, finish] if tree else [add_row]
    queue = []

    def advance():
        while len(queue) < len(g_copies):
            queue.append(0)
        moves = []
        for i, (l, n, cp) in enumerate(g_copies):
            if queue[i] < len(stages):
                moves.append((stages[queue[i]], l, n, cp))
                queue[i] += 1
        for f, l, n, cp in moves:
            f(l, n, cp)
        return len(moves)

    small[...] = jnp.zeros_like(small)
    for l in reversed(range(layers)):
        ph = 4 * l + 2
        gf = (g * modrow(l, 5)).astype(BF16)
        copies = gather_start(ph, gf)
        small[l * 6 + 5:l * 6 + 6, :] = col_sum(g * feed[l])
        small[12 + l:13 + l, :] = col_sum(gf.astype(F32))
        slope = gelu_slope(before[l])
        advance()
        gf_all = gather_end(ph, copies)
        ga = dot(gf_all[:, :half], wd[l, 0], 1, 1) + dot(gf_all[:, half:], wd[l, 1], 1, 1)
        gb = (ga * slope).astype(BF16)
        copies = scatter_start(ph, [dot(gb, wu[l, j], 1, 1) for j in range(n_row)])
        a = act[l]
        for j in range(n_row):
            gd_s[l, j] = dot(a, gf_all[:, j * half:(j + 1) * half], 0, 0).astype(BF16)
        grad_send(l, 3)
        small[16 + l:17 + l, :] = col_sum(gb.astype(F32))
        hid2 = gathered(4 * l + 1)
        for j in range(n_row):
            gu_s[l, j] = dot(hid2[:, j * half:(j + 1) * half], gb, 0, 0).astype(BF16)
        grad_send(l, 2)
        gh = scatter_end(ph, copies)
        normed = n2[l]
        gm = g + norm_back(gh * (1.0 + modrow(l, 4)), normed, i2[l])
        gattn = (gm * modrow(l, 2)).astype(BF16)
        ph = 4 * l + 3
        copies = gather_start(ph, gattn)
        small[l * 6 + 4:l * 6 + 5, :] = col_sum(gh * normed)
        small[l * 6 + 3:l * 6 + 4, :] = col_sum(gh)
        small[l * 6 + 2:l * 6 + 3, :] = col_sum(gm * attn[l])
        small[14 + l:15 + l, :] = col_sum(gattn.astype(F32))
        ga_all = gather_end(ph, copies)
        gmix = (
            dot(ga_all[:, :half], wo[l, 0], 1, 1) + dot(ga_all[:, half:], wo[l, 1], 1, 1)
        ).astype(BF16)
        scale = HEAD ** (-0.5)
        for h in range(n_heads):
            lo = h * HEAD
            q = proj[l, :, lo:lo + HEAD]
            kk = proj[l, :, heads_w + lo:heads_w + lo + HEAD]
            vv = proj[l, :, 2 * heads_w + lo:2 * heads_w + lo + HEAD]
            gh_ = gmix[:, lo:lo + HEAD]
            soft = softmax_parts(q, kk)
            gs = dot(gh_, vv, 1, 1)
            gsc = (soft * (gs - jnp.sum(soft * gs, axis=-1, keepdims=True))).astype(BF16)
            gat[:, lo:lo + HEAD] = (dot(gsc, kk) * scale).astype(BF16)
            gat[:, heads_w + lo:heads_w + lo + HEAD] = (dot(gsc, q, 0, 0) * scale).astype(BF16)
            gat[:, 2 * heads_w + lo:2 * heads_w + lo + HEAD] = dot(soft.astype(BF16), gh_, 0, 0).astype(BF16)
        gp = gat[...]
        copies = scatter_start(ph, [dot(gp, wq[l, j], 1, 1) for j in range(n_row)])
        advance()
        hid1 = gathered(4 * l)
        for j in range(n_row):
            gq_s[l, j] = dot(hid1[:, j * half:(j + 1) * half], gp, 0, 0).astype(BF16)
        grad_send(l, 0)
        m = mix[l]
        for j in range(n_row):
            go_s[l, j] = dot(m, ga_all[:, j * half:(j + 1) * half], 0, 0).astype(BF16)
        grad_send(l, 1)
        small[18 + l:19 + l, :gp.shape[1]] = col_sum(gp.astype(F32))
        if l == 0:
            advance()
        gh = scatter_end(ph, copies)
        normed = n1[l]
        small[l * 6 + 1:l * 6 + 2, :] = col_sum(gh * normed)
        small[l * 6:l * 6 + 1, :] = col_sum(gh)
        g = gm + norm_back(gh * (1.0 + modrow(l, 1)), normed, i1[l])
    tg_copies = spread(1, g.astype(BF16), 1, tok_grad)
    out = []
    for k in range(1, n_col):
        where = {"row": r, "col": lax.rem(c + k, n_col)}
        out.append(remote(small.at[:16], col_r.at[k - 1], c_send.at[k], c_recv.at[k], where))
    advance()
    total = small[:16]
    for k, cp in enumerate(out):
        cp.wait_recv()
        total = total + col_r[k]
    low = jnp.concatenate([small[16:24], cond[r]], axis=0)
    tab_s[...] = jnp.concatenate([total, low], axis=0).astype(BF16)
    me = d * n_row + r
    out = []
    for k in range(1, line):
        to = lax.rem(me + k, line)
        where = {"dp": to // n_row, "row": lax.rem(to, n_row)}
        out.append(remote(tab_s, table.at[me], d_send.at[k], d_recv.at[k], where))
    table[me] = tab_s[...]
    advance()
    for cp in out:
        cp.wait_recv()
    while advance():
        pass
    spread_end(res_copies, 0, result)
    spread_end(tg_copies, 1, tok_grad)
    for cp in pending:
        cp.wait_send()


def run_blocks(n_dp, n_row, n_col, tokens, cotangent, mod_part, cond, w_qkv, w_out, w_up, w_down, b_qkv, b_up):
    layers, half, qkv_w = w_qkv.shape
    full = tokens.shape[1]
    chunk = full // n_col
    width = half * n_row
    head_w = w_out.shape[1]
    hid = w_up.shape[2]
    any_spec = pl.BlockSpec(memory_space=pl.ANY)
    vmem = pl.BlockSpec(memory_space=pltpu.VMEM)
    group = n_row * n_col
    out_shape = (
        jax.ShapeDtypeStruct((n_row, n_col, chunk, half), BF16),
        jax.ShapeDtypeStruct((n_row, n_col, chunk, half), BF16),
        jax.ShapeDtypeStruct((layers, half, qkv_w), BF16),
        jax.ShapeDtypeStruct((layers, head_w, half), BF16),
        jax.ShapeDtypeStruct((layers, half, hid), BF16),
        jax.ShapeDtypeStruct((layers, hid, half), BF16),
        jax.ShapeDtypeStruct((n_dp * n_row, 32, width), BF16),
    )
    dma = pltpu.SemaphoreType.DMA
    v = pltpu.VMEM
    phases = 4 * layers
    grads = [(layers, half, qkv_w), (layers, head_w, half), (layers, half, hid), (layers, hid, half)]
    scratch = [
        v((24, width), F32),
        v((n_col - 1, 16, width), F32),
        v((32, width), BF16),
        v((layers, n_row, half, qkv_w), BF16),
        v((layers, n_row, head_w, half), BF16),
        v((layers, n_row, half, hid), BF16),
        v((layers, n_row, hid, half), BF16),
        v((n_row, chunk, half), BF16),
        v((n_row, chunk, half), BF16),
        v((n_row, n_col) + mod_part.shape[1:], F32),
        v((mod_part.shape[1], width), F32),
        v((phases, n_col, chunk, width), BF16),
        v((phases, n_col - 1, chunk, width), BF16),
        v((phases, n_col, chunk, width), BF16),
        v((16, 128), BF16),
        v((full, qkv_w), BF16),
        v((layers, full, qkv_w), BF16),
        v((layers, full, head_w), BF16),
        v((layers, chunk, width), F32),
        v((layers, chunk, width), F32),
        v((layers, chunk, 1), F32),
        v((layers, chunk, width), F32),
        v((layers, chunk, 1), F32),
        v((layers, full, hid), F32),
        v((layers, full, hid), BF16),
        v((layers, chunk, width), F32),
        v((layers, chunk, width), F32),
        v((layers, n_row, half, qkv_w), BF16),
        v((layers, n_row, head_w, half), BF16),
        v((layers, n_row, half, hid), BF16),
        v((layers, n_row, hid, half), BF16),
        v((layers, half, qkv_w), BF16),
        v((layers, head_w, half), BF16),
        v((layers, half, hid), BF16),
        v((layers, hid, half), BF16),
        *[v(g, BF16) for g in grads * 3],
        v((2, n_row, chunk, half), BF16),
        v((2, n_row, n_col, chunk, half), BF16),
        dma((2 * phases, n_col)),
        dma((2 * phases, n_col)),
        dma((4 * layers,)),
        dma((4 * layers,)),
        dma((4 * layers,)),
        dma((8 * layers,)),
        dma((8 * layers,)),
        dma((3, group)),
        dma((3, group)),
        dma((2,)),
        dma((2,)),
        dma((2,)),
        dma((8 * layers, 3)),
        dma((8 * layers, 3)),
        dma((n_col,)),
        dma((n_col,)),
        dma((n_dp * n_row,)),
        dma((n_dp * n_row,)),
    ]
    return pl.pallas_call(
        functools.partial(block_kernel, layers, n_dp, n_row, n_col),
        out_shape=out_shape,
        in_specs=[any_spec, any_spec, vmem, vmem, any_spec, any_spec, any_spec, any_spec, vmem, vmem],
        out_specs=tuple([vmem] * 7),
        scratch_shapes=scratch,
        compiler_params=pltpu.CompilerParams(
            collective_id=0, has_side_effects=True, vmem_limit_bytes=58 * 1024 * 1024
        ),
        name="blocks",
    )(tokens, cotangent, mod_part, cond, w_qkv, w_out, w_up, w_down, b_qkv, b_up)


def local(n_dp, n_row, n_col, tokens, condition, cotangent, w_ada, b_ada, w_qkv, b_qv, w_out, b_out,
          up_weight, up_bias, down_weight, down_bias):
    layers = w_ada.shape[0]
    half = tokens.shape[2]
    latents = tokens.shape[0]
    r = lax.axis_index("row")
    c = lax.axis_index("col")
    d = lax.axis_index("dp")
    cond_float = condition.astype(F32)
    cond_low = silu_plain(cond_float).astype(BF16)
    part = jnp.einsum("lc,nckd->lnkd", cond_low, w_ada, preferred_element_type=F32)
    part = part + jnp.where(c == 0, b_ada.astype(F32), 0.0)[None]
    biases = jnp.where(c == 0, jnp.concatenate([b_out, down_bias]).astype(F32), 0.0)
    biases = jnp.broadcast_to(biases[None], (latents,) + biases.shape)
    part = jnp.concatenate([part.reshape(latents, layers * 6, half), biases], axis=1)
    cond_rows = jnp.pad(
        cond_low.astype(F32)[:, None], ((0, 0), (0, 7), (0, n_row * half - condition.shape[1]))
    )
    bq = b_qv.astype(F32)
    b_qkv = jnp.concatenate([bq[:, 0], jnp.zeros_like(bq[:, 0]), bq[:, 1]], axis=1)
    q_w = w_qkv.shape[3]
    res, tg, g_qkv, g_out, g_up, g_down, table = run_blocks(
        n_dp, n_row, n_col, tokens, cotangent, part, cond_rows, w_qkv.reshape(layers, half, 3 * q_w), w_out, up_weight,
        down_weight, b_qkv, up_bias.astype(F32),
    )
    sums = (g_qkv, g_out, g_up, g_down)
    if n_dp != 4:
        sums = lax.psum(sums, "dp")
    g_qkv, g_out, g_up, g_down = [t.astype(F32) for t in sums]
    cond_all = table[:, 24, : cond_low.shape[1]]
    mine = lax.dynamic_slice_in_dim(table[:, :16], r * half, half, axis=2)
    gmod = mine[:, :12].reshape(-1, layers, 6, half)
    w_ada_grad = jnp.einsum("lc,lnkd->nckd", cond_all, gmod, preferred_element_type=F32)
    b_ada_grad = jnp.sum(gmod, axis=0, dtype=F32)
    own = lax.dynamic_slice_in_dim(gmod, d * latents, latents, axis=0)
    cond_term = lax.psum(jnp.einsum("lnkd,nckd->lc", own, w_ada, preferred_element_type=F32), "row")
    condition_grad = jax.vjp(silu_plain, cond_float)[1](cond_term)[0].astype(BF16)
    vec = jnp.sum(mine[:, 12:16], axis=0, dtype=F32)
    rest = jnp.sum(table[:, 16:20], axis=0, dtype=F32)
    b_qkv_g = rest[2:4, : 3 * q_w].reshape(layers, 3, q_w)
    return (
        res.reshape(tokens.shape),
        tg.reshape(tokens.shape),
        condition_grad,
        w_ada_grad,
        b_ada_grad,
        g_qkv.reshape(w_qkv.shape),
        jnp.stack([b_qkv_g[:, 0], b_qkv_g[:, 2]], axis=1),
        g_out,
        vec[2:4],
        g_up,
        rest[0:2],
        g_down,
        vec[0:2],
    )


def solution(mesh):
    in_specs = (
        P("dp", None, "row"),
        P("dp", "col"),
        P("dp", None, "row"),
        P(None, "col", None, "row"),
        P(None, None, "row"),
        P(None, "row", None, "col"),
        P(None, None, "col"),
        P(None, "col", "row"),
        P(None, "row"),
        P(None, "row", "col"),
        P(None, "col"),
        P(None, "col", "row"),
        P(None, "row"),
    )
    out_specs = (
        P("dp", None, "row"),
        P("dp", None, "row"),
        P("dp", "col"),
        P(None, "col", None, "row"),
        P(None, None, "row"),
        P(None, "row", None, "col"),
        P(None, None, "col"),
        P(None, "col", "row"),
        P(None, "row"),
        P(None, "row", "col"),
        P(None, "col"),
        P(None, "col", "row"),
        P(None, "row"),
    )
    sizes = [mesh.shape[a] for a in ("dp", "row", "col")]
    return jax.shard_map(
        functools.partial(local, *sizes), mesh=mesh, in_specs=in_specs, out_specs=out_specs, check_vma=False
    )
```
